256 devices in a mesh: dp: 8 (over x, y_lo), owner: 32 (over z, y_hi, core).
Axes of the slice: x: 4, y: 4 (y_hi: 2, y_lo: 2; y = y_hi * 2 + y_lo), z: 8, core: 2. Of those that a mesh axis runs over, the one named last changes fastest.
Arguments:
- grad_parts: bfloat16 [8, 256, 512, 512], P('dp', None, 'owner'), may hold values from -6 to 6
- owner_of: int32 [256], replicated, may hold values from 0 to 255, as said below
- refresh: int32 [32], replicated, may hold values from 0 to 255, as said below
- left_stat: float32 [256, 512, 512], P(('dp', 'owner')), may hold values from -0.05 to 0.1, as said below
- right_stat: float32 [256, 512, 512], P(('dp', 'owner')), may hold values from -0.05 to 0.1, as said below
- left_root: float32 [256, 512, 512], P(('dp', 'owner')), may hold values from -1 to 4, as said below
- right_root: float32 [256, 512, 512], P(('dp', 'owner')), may hold values from -1 to 4, as said below
Outputs:
- update: bfloat16 [256, 512, 512], P(('dp', 'owner'))
- new_left_stat: float32 [256, 512, 512], P(('dp', 'owner'))
- new_right_stat: float32 [256, 512, 512], P(('dp', 'owner'))
- new_left_root: float32 [256, 512, 512], P(('dp', 'owner'))
- new_right_root: float32 [256, 512, 512], P(('dp', 'owner'))
The draws below stay inside these ranges and needn't reach their ends.
Inputs may be any that keep to these rules, and one draw needn't show every extreme that they name: `owner_of`: A permutation of the blocks over the device slots. `refresh`: 32 distinct blocks; no two of them are owned by the slots 2 k and 2 k + 1 for any k. `left_stat`: each block symmetric positive definite. `right_stat`: each block symmetric positive definite. `left_root`: each block symmetric positive definite. `right_root`: each block symmetric positive definite.
All inputs are finite; a program needn't handle non-finite values.
Results may differ from the reference program's by a relative error of at most 0.034.
Values may be sent and summed in bfloat16 or wider, within the bound.
No kernel may reach another device: no remote copies, remote signals or barrier semaphores. Data moves between devices by JAX's collectives and lax.ppermute only.
A program may use at most 64 MiB of HBM per device.

```python
import math
import jax
import jax.numpy as jnp
from jax import lax

B = 512
ITERS = 3
NB = 256
NREF = 32
N_DP = 8


def gram_blocks(key, shift, low_end, high_end, overall):
    key_g, key_d = jax.random.split(key, 2)
    factors = jax.random.normal(key_g, (NB, B, B), jnp.float32)
    gram = jnp.einsum('nik,njk->nij', factors, factors, precision=lax.Precision.HIGHEST) / B
    gram = 0.5 * (gram + jnp.swapaxes(gram, 1, 2))
    identity = jnp.eye(B, dtype=jnp.float32)
    gram = gram + shift * identity
    scales = jnp.exp(jax.random.uniform(key_d, (NB, B, 1), jnp.float32, math.log(low_end), math.log(high_end)))
    return overall * scales * gram * jnp.swapaxes(scales, 1, 2)


def owner_table(key):
    table = jax.random.permutation(jax.random.fold_in(key, 101), NB).astype(jnp.int32)
    first_slot = table[0]
    last_slot = table[NB - 1]
    clash = first_slot // 2 == last_slot // 2
    second_slot = table[1]
    table = table.at[0].set(jnp.where(clash, second_slot, first_slot))
    table = table.at[1].set(jnp.where(clash, first_slot, second_slot))
    return table.astype(jnp.int32)


def draw_owner_of(key, part):
    return owner_table(key)


def draw_refresh(key, part):
    owner_tab = owner_table(key)
    key = jax.random.fold_in(key, 7)
    key_pair, key_bit, key_order = jax.random.split(key, 3)
    pair_count = NB // 2
    slot_last = owner_tab[NB - 1]
    slot_first = owner_tab[0]
    pair_ids = jnp.arange(pair_count, dtype=jnp.int32)
    ranks = jnp.argsort(jax.random.permutation(key_pair, pair_count).astype(jnp.int32)).astype(jnp.int32)
    ranks = jnp.where(pair_ids == slot_last // 2, -2, ranks)
    ranks = jnp.where(pair_ids == slot_first // 2, -1, ranks)
    chosen_pairs = jnp.argsort(ranks, stable=True)[:NREF].astype(jnp.int32)
    chosen_bits = jax.random.randint(key_bit, (NREF,), 0, 2).astype(jnp.int32)
    chosen_bits = jnp.where(chosen_pairs == slot_last // 2, slot_last % 2, chosen_bits)
    chosen_bits = jnp.where(chosen_pairs == slot_first // 2, slot_first % 2, chosen_bits)
    chosen_slots = chosen_pairs * 2 + chosen_bits
    block_at = jnp.argsort(owner_tab).astype(jnp.int32)
    blocks = block_at[chosen_slots].astype(jnp.int32)
    order = jax.random.permutation(key_order, NREF)
    return blocks[order].astype(jnp.int32)


def draw_left_stat(key, part):
    key = jax.random.fold_in(key, 3)
    return gram_blocks(key, 0.05, 0.4, 1.6, 1.0 / 128.0)


def draw_right_stat(key, part):
    key = jax.random.fold_in(key, 4)
    return gram_blocks(key, 0.05, 0.4, 1.6, 1.0 / 128.0)


def draw_left_root(key, part):
    key = jax.random.fold_in(key, 5)
    return gram_blocks(key, 0.3, 0.5, 1.4, 0.5)


def draw_right_root(key, part):
    key = jax.random.fold_in(key, 6)
    return gram_blocks(key, 0.3, 0.5, 1.4, 0.5)


def levels(key, dims, cuts, smallest, top_value):
    loudness = 1.0
    for dim, blocks in cuts:
        draws = jax.random.uniform(jax.random.fold_in(jax.random.fold_in(key, 6), dim), (blocks,), jnp.float32, smallest / len(cuts), top_value / len(cuts))
        loudness = loudness * jnp.repeat(jnp.exp(draws), dims[dim] // blocks).reshape((-1,) + (1,) * (len(dims) - 1 - dim))
    return loudness


def centred(key, dims, deviation, most, cuts=(), kind=jnp.bfloat16):
    array = jax.random.normal(key, dims, jnp.float32) * deviation
    if len(cuts) > 0:
        array = levels(key, dims, cuts, -0.22, 0.18) * array
    return jnp.clip(array, min=-most, max=most).astype(kind)


def setup_inputs(seed: int = 0) -> dict:
    key_of = jax.random.split(jax.random.key(seed), 8)
    return {
        "grad_parts": centred(key_of[0], (N_DP, NB, B, B), 0.4, 6.0, ((0, 8), (2, 32))),
        "owner_of": draw_owner_of(jax.random.fold_in(key_of[7], 71), 0),
        "refresh": draw_refresh(jax.random.fold_in(key_of[7], 71), 0),
        "left_stat": draw_left_stat(jax.random.fold_in(key_of[7], 71), 0),
        "right_stat": draw_right_stat(jax.random.fold_in(key_of[7], 71), 0),
        "left_root": draw_left_root(jax.random.fold_in(key_of[7], 71), 0),
        "right_root": draw_right_root(jax.random.fold_in(key_of[7], 71), 0),
    }


DECAY = 0.9
SHARE = 0.1

def inverse_root(matrix):
    highest = lax.Precision.HIGHEST
    identity = jnp.eye(matrix.shape[0], dtype=jnp.float32)
    frob_norm = jnp.sqrt(jnp.sum(matrix * matrix))
    iterate = matrix / frob_norm
    inverse = identity
    for sweep_index in range(ITERS):
        factor = (5.0 * identity - iterate) * 0.25
        if sweep_index == 0:
            inverse = factor * lax.rsqrt(jnp.sqrt(frob_norm))
        else:
            inverse = jnp.dot(inverse, factor, precision=highest)
        if sweep_index + 1 < ITERS:
            powered = jnp.dot(factor, factor, precision=highest)
            powered = jnp.dot(powered, factor, precision=highest)
            powered = jnp.dot(powered, factor, precision=highest)
            iterate = jnp.dot(powered, iterate, precision=highest)
    return inverse

def reference(grad_parts, owner_of, refresh, left_stat, right_stat, left_root, right_root):
    block_count = owner_of.shape[0]
    block_at = jnp.zeros((block_count,), jnp.int32).at[owner_of].set(jnp.arange(block_count, dtype=jnp.int32))

    def one_slot(slot_index):
        block_id = block_at[slot_index].astype(jnp.int32)
        partials = lax.dynamic_index_in_dim(grad_parts, block_id, 1, keepdims=False)
        gradient = lax.optimization_barrier(jnp.sum(partials.astype(jnp.float32), axis=0)).astype(jnp.bfloat16)
        width = gradient.shape[0]
        left_old = lax.dynamic_index_in_dim(left_stat, slot_index, 0, keepdims=False)
        right_old = lax.dynamic_index_in_dim(right_stat, slot_index, 0, keepdims=False)
        left_prev = lax.dynamic_index_in_dim(left_root, slot_index, 0, keepdims=False)
        right_prev = lax.dynamic_index_in_dim(right_root, slot_index, 0, keepdims=False)
        coeff = SHARE / width
        new_left = DECAY * left_old + coeff * jnp.dot(gradient, gradient.T, preferred_element_type=jnp.float32)
        new_right = DECAY * right_old + coeff * jnp.dot(gradient.T, gradient, preferred_element_type=jnp.float32)
        left_low = left_prev.astype(jnp.bfloat16)
        right_low = right_prev.astype(jnp.bfloat16)
        left_part = jnp.dot(left_low, gradient, preferred_element_type=jnp.float32).astype(jnp.bfloat16)
        update = jnp.dot(left_part, right_low, preferred_element_type=jnp.float32).astype(jnp.bfloat16)
        refreshed = jnp.any(refresh == block_id)
        fresh_left, fresh_right = lax.cond(refreshed, lambda: (inverse_root(left_old), inverse_root(right_old)), lambda: (left_prev, right_prev))
        return (update, new_left, new_right, fresh_left, fresh_right)
    outputs = lax.map(one_slot, jnp.arange(block_count, dtype=jnp.int32))
    return (outputs[0], outputs[1], outputs[2], outputs[3], outputs[4])
```

```python
import functools

import jax
import jax.numpy as jnp
import numpy as np
from jax import lax
from jax.experimental import pallas as pl
from jax.experimental.pallas import tpu as pltpu
from jax.sharding import PartitionSpec as P

DECAY = 0.9
SHARE = 0.1
AXES = ("dp", "owner")
MIB = 1 << 20

ORDERS = {0: (("a", "y", "b"), ("y", "b", "a")), 1: (("b", "a", "y"), ("y", "b", "a"))}


def split_slot(slot, n_owner):
    data, owner = divmod(slot, n_owner)
    return data // 2, data % 2, owner


def join_slot(x, y_lo, owner, n_owner):
    return (x * 2 + y_lo) * n_owner + owner


def flip(slot, dim, n_owner):
    x, y_lo, owner = split_slot(slot, n_owner)
    if dim == "a":
        x ^= 1
    elif dim == "b":
        x ^= 3
    else:
        y_lo ^= 1
    return join_slot(x, y_lo, owner, n_owner)


def exchange(n_slots, n_owner, part, step):
    return [(s, flip(s, ORDERS[s % 2][part][step], n_owner)) for s in range(n_slots)]


def slot_rows(n_slots, n_owner, cuts):
    rows = np.zeros((n_slots, 2, n_slots // 2), np.int32)
    for s in range(n_slots):
        x, y_lo, _ = split_slot(s, n_owner)
        for kind, first in ((0, 1), (1, 0)):
            out = []
            for part in range(2):
                one, two, three = ORDERS[s % 2][part]
                for second in (0, 1):
                    for third in (0, 1):
                        for owner in range(cuts[part], cuts[part + 1]):
                            t = join_slot(x, y_lo, owner, n_owner)
                            for dim, bit in ((one, first), (two, second), (three, third)):
                                t = flip(t, dim, n_owner) if bit else t
                            out.append(t)
            rows[s, kind] = out
    return rows


def pick_kernel(owner_ref, slots_ref, shard_ref, first_ref, second_ref, held, block_at, sem):
    copy = pltpu.make_async_copy(shard_ref, held, sem)
    copy.start()

    @pl.loop(0, owner_ref.shape[0], unroll=8)
    def _(b):
        block_at[owner_ref[b]] = b

    copy.wait()
    offset = 0
    for out in (first_ref, second_ref):

        @pl.loop(0, out.shape[0], unroll=4)
        def _(i, out=out, offset=offset):
            out[i] = held[block_at[slots_ref[offset + i]]]

        offset += out.shape[0]


def pick(owner_of, slots, shard_rows, counts):
    _, rows, width = shard_rows.shape
    vmem = pl.BlockSpec(memory_space=pltpu.VMEM)
    smem = pl.BlockSpec(memory_space=pltpu.SMEM)
    return pl.pallas_call(
        pick_kernel,
        out_shape=[jax.ShapeDtypeStruct((n, rows, width), shard_rows.dtype) for n in counts],
        in_specs=[smem, smem, pl.BlockSpec(memory_space=pl.ANY)],
        out_specs=[vmem] * 2,
        scratch_shapes=[
            pltpu.VMEM(shard_rows.shape, shard_rows.dtype),
            pltpu.SMEM(owner_of.shape, jnp.int32),
            pltpu.SemaphoreType.DMA,
        ],
        compiler_params=pltpu.CompilerParams(vmem_limit_bytes=16 * MIB),
        cost_estimate=pl.CostEstimate(flops=0, bytes_accessed=12 * MIB, transcendentals=0),
    )(owner_of, slots, shard_rows)


def times(a, b):
    return jnp.dot(
        a.astype(jnp.bfloat16), b.astype(jnp.bfloat16), preferred_element_type=jnp.float32
    )


def next_iterate(m):
    d = (times(m, m) - 10.0 * m) * (1.0 / 16.0)
    e = times(d, d) + 3.125 * d
    return (625.0 / 256.0) * m + times(e, m)


def root_of(stat):
    c = jnp.sqrt(jnp.sum(stat * stat))
    m0 = stat / c
    m1 = next_iterate(m0)
    m2 = next_iterate(m1)
    t = times(m0, m1)
    pair = m0 + m1
    total = times(5.0 * pair - t, m2) + 5.0 * t - 25.0 * (pair + m2)
    n = stat.shape[0]
    on_diagonal = lax.broadcasted_iota(jnp.int32, (n, n), 0) == lax.broadcasted_iota(
        jnp.int32, (n, n), 1
    )
    total = total + jnp.where(on_diagonal, 125.0, 0.0)
    return total * (lax.rsqrt(jnp.sqrt(c)) * (1.0 / 64.0))


def roots_kernel(owner_ref, refresh_ref, slot_ref, stat_ref, root_ref, out_ref):
    slot = slot_ref[0]

    def look(i, found):
        return found | jnp.where(owner_ref[refresh_ref[i]] == slot, 1, 0)

    fresh = lax.fori_loop(0, refresh_ref.shape[0], look, jnp.int32(0))

    @pl.when(fresh == 1)
    def _():
        out_ref[...] = root_of(stat_ref[...])

    @pl.when(fresh == 0)
    def _():
        out_ref[...] = root_ref[...]


def roots(owner_of, refresh, slot, stat, root):
    vmem = pl.BlockSpec(memory_space=pltpu.VMEM)
    smem = pl.BlockSpec(memory_space=pltpu.SMEM)
    return pl.pallas_call(
        roots_kernel,
        out_shape=jax.ShapeDtypeStruct(stat.shape, stat.dtype),
        in_specs=[smem, smem, smem, vmem, vmem],
        out_specs=vmem,
        compiler_params=pltpu.CompilerParams(vmem_limit_bytes=32 * MIB),
        cost_estimate=pl.CostEstimate(flops=8 * 2 * 512**3, bytes_accessed=3 * MIB, transcendentals=0),
    )(owner_of, refresh, slot, stat, root)


def finish_kernel(grad_ref, ls_ref, rs_ref, lr_ref, rr_ref, up_ref, nl_ref, nr_ref):
    grad = grad_ref[...]
    coeff = SHARE / grad.shape[1]
    f32 = jnp.float32
    left_part = jnp.dot(lr_ref[...].astype(jnp.bfloat16), grad, preferred_element_type=f32)
    up_ref[...] = jnp.dot(
        left_part.astype(jnp.bfloat16),
        rr_ref[...].astype(jnp.bfloat16),
        preferred_element_type=f32,
    ).astype(jnp.bfloat16)
    gram = lax.dot_general(grad, grad, (((1,), (1,)), ((), ())), preferred_element_type=f32)
    nl_ref[...] = DECAY * ls_ref[...] + coeff * gram
    gram = lax.dot_general(grad, grad, (((0,), (0,)), ((), ())), preferred_element_type=f32)
    nr_ref[...] = DECAY * rs_ref[...] + coeff * gram


def finish(grad, left_stat, right_stat, left_root, right_root):
    vmem = pl.BlockSpec(memory_space=pltpu.VMEM)
    return pl.pallas_call(
        finish_kernel,
        out_shape=[
            jax.ShapeDtypeStruct(grad.shape, jnp.bfloat16),
            jax.ShapeDtypeStruct(left_stat.shape, jnp.float32),
            jax.ShapeDtypeStruct(right_stat.shape, jnp.float32),
        ],
        in_specs=[vmem] * 5,
        out_specs=[vmem] * 3,
        compiler_params=pltpu.CompilerParams(vmem_limit_bytes=32 * MIB),
        cost_estimate=pl.CostEstimate(flops=4 * 2 * 512**3, bytes_accessed=7 * MIB, transcendentals=0),
    )(grad, left_stat, right_stat, left_root, right_root)


def plus(a, b):
    return (a.astype(jnp.float32) + b.astype(jnp.float32)).astype(jnp.bfloat16)


def per_device(grad_parts, owner_of, refresh, left_stat, right_stat, left_root, right_root):
    n_owner = lax.axis_size("owner")
    n_slots = lax.axis_size("dp") * n_owner
    my_slot = lax.axis_index("dp") * n_owner + lax.axis_index("owner")
    shard_rows = grad_parts[0]
    cuts = (0, (2 * n_owner) // 3, n_owner)
    table = slot_rows(n_slots, n_owner, cuts)
    mine = lax.dynamic_index_in_dim(jnp.asarray(table), my_slot, 0, keepdims=False)
    counts = [4 * (cuts[1] - cuts[0]), 4 * (cuts[2] - cuts[1])]
    sent = pick(owner_of, mine[0], shard_rows, counts)
    kept = pick(owner_of, mine[1], shard_rows, counts)
    summed = []
    for step in range(3):
        arrived = [
            lax.ppermute(s, AXES, exchange(n_slots, n_owner, part, step))
            for part, s in enumerate(sent)
        ]
        if step == 2:
            summed = [plus(a, k) for a, k in zip(arrived, kept)]
        else:
            half = [a.shape[0] // 2 for a in arrived]
            sent = [plus(a[h:], k[h:]) for a, k, h in zip(arrived, kept, half)]
            kept = [plus(a[:h], k[:h]) for a, k, h in zip(arrived, kept, half)]
    outgoing = jnp.concatenate(summed, axis=0)
    grad = lax.all_to_all(outgoing, "owner", split_axis=0, concat_axis=0, tiled=True)
    grad = grad.reshape(left_stat.shape[1], -1)
    slot = my_slot.reshape(1)
    new_left_root = roots(owner_of, refresh, slot, left_stat[0], left_root[0])
    new_right_root = roots(owner_of, refresh, slot, right_stat[0], right_root[0])
    update, new_left, new_right = finish(
        grad, left_stat[0], right_stat[0], left_root[0], right_root[0]
    )
    return (
        update[None],
        new_left[None],
        new_right[None],
        new_left_root[None],
        new_right_root[None],
    )


def solution(mesh):
    owned = P(AXES, None, None)
    return jax.shard_map(
        per_device,
        mesh=mesh,
        in_specs=(P("dp", None, "owner", None), P(), P(), owned, owned, owned, owned),
        out_specs=(owned,) * 5,
        check_vma=False,
    )
```

```python
import functools

import jax
import jax.numpy as jnp
import numpy as np
from jax import lax
from jax.experimental import pallas as pl
from jax.experimental.pallas import tpu as pltpu
from jax.sharding import PartitionSpec as P

DECAY = 0.9
SHARE = 0.1
AXES = ("dp", "owner")
MIB = 1 << 20

QUAD = ((0, 0), (0, 1), (1, 0), (1, 1))
WIDE = {0: ("a", "y", "b"), 1: ("b", "a", "y")}
SLIM = {0: ("y", "b", "a"), 1: ("y", "b", "a")}
STREAMS = {
    "far": ((3, 5), WIDE),
    "farthest": ((4,), SLIM),
    "middle": ((2, 6), WIDE),
    "near": ((1, 7), WIDE),
    "here": ((0,), SLIM),
}


def place(slot, n_owner):
    data, owner = divmod(slot, n_owner)
    return data // 2, 2 * ((owner // 2) % 2) + data % 2, owner // 4, owner % 2


def slot_at(x, y, z, core, n_owner):
    return (2 * x + y % 2) * n_owner + 4 * (z % (n_owner // 4)) + 2 * (y // 2) + core


def moved(slot, n_owner, dims="", rz=0, yb=0, rc=0):
    x, y, z, core = place(slot, n_owner)
    x ^= ("a" in dims) * 1 ^ ("b" in dims) * 3
    y ^= ("y" in dims) * 1 ^ yb * 3
    return slot_at(x, y, z + rz, core ^ rc, n_owner)


def route(n_slots, n_owner, **how):
    return [(s, moved(s, n_owner, **how)) for s in range(n_slots)]


def route_step(n_slots, n_owner, orders, step):
    return [
        (s, moved(s, n_owner, dims=orders[place(s, n_owner)[3]][step])) for s in range(n_slots)
    ]


def owners_of_pieces(slot, n_owner, rzs, orders, first):
    one, two, three = orders[place(slot, n_owner)[3]]
    out = []
    for second in (0, 1):
        for third in (0, 1):
            dims = one * first + two * second + three * third
            for rz in rzs:
                for yb, rc in QUAD:
                    out.append(moved(slot, n_owner, dims=dims, rz=rz, yb=yb, rc=rc))
    return out


def build_table(n_slots, n_owner):
    spans, rows = {}, []
    for s in range(n_slots):
        row = []
        for name, (rzs, orders) in STREAMS.items():
            groups = [((name, rz), (rz,)) for rz in rzs] if name == "near" else [(name, rzs)]
            for key, group in groups:
                for first in (1, 0):
                    pieces = owners_of_pieces(s, n_owner, group, orders, first)
                    spans[key, first] = (len(row), len(pieces))
                    row += pieces
        rows.append(row)
    return spans, np.asarray(rows, np.int32)


def index_kernel(owner_ref, slots_ref, out_ref, block_at):
    @pl.loop(0, owner_ref.shape[0], unroll=8)
    def _(b):
        block_at[owner_ref[b]] = b

    @pl.loop(0, slots_ref.shape[0], unroll=8)
    def _(i):
        out_ref[i] = block_at[slots_ref[i]]


def index_pieces(owner_of, slots):
    smem = pl.BlockSpec(memory_space=pltpu.SMEM)
    return pl.pallas_call(
        index_kernel,
        out_shape=jax.ShapeDtypeStruct(slots.shape, jnp.int32),
        in_specs=[smem, smem],
        out_specs=smem,
        scratch_shapes=[pltpu.SMEM(owner_of.shape, jnp.int32)],
    )(owner_of, slots)


def pick_kernel(spans, n_after, index_ref, shard_ref, *refs):
    for out, pieces in zip(refs[n_after:], spans):
        offset = 0
        for start, count in pieces:

            @pl.loop(0, count, unroll=4)
            def _(i, out=out, offset=offset, start=start):
                out[offset + i] = shard_ref[index_ref[start + i]]

            offset += count


def pick(index, shard_rows, spans, after=()):
    _, rows, width = shard_rows.shape
    vmem = pl.BlockSpec(memory_space=pltpu.VMEM)
    counts = [sum(n for _, n in pieces) for pieces in spans]
    return pl.pallas_call(
        functools.partial(pick_kernel, spans, len(after)),
        out_shape=[jax.ShapeDtypeStruct((n, rows, width), shard_rows.dtype) for n in counts],
        in_specs=[pl.BlockSpec(memory_space=pltpu.SMEM), vmem]
        + [pl.BlockSpec(memory_space=pl.ANY)] * len(after),
        out_specs=[vmem] * len(counts),
        compiler_params=pltpu.CompilerParams(vmem_limit_bytes=16 * MIB),
        cost_estimate=pl.CostEstimate(
            flops=0, bytes_accessed=2 * sum(counts) * rows * width * 2, transcendentals=0
        ),
    )(index, shard_rows, *after)


def times(a, b):
    return jnp.dot(
        a.astype(jnp.bfloat16), b.astype(jnp.bfloat16), preferred_element_type=jnp.float32
    )


def next_iterate(m):
    d = (times(m, m) - 10.0 * m) * (1.0 / 16.0)
    e = times(d, d) + 3.125 * d
    return (625.0 / 256.0) * m + times(e, m)


def root_of(stat):
    c = jnp.sqrt(jnp.sum(stat * stat))
    m0 = stat / c
    m1 = next_iterate(m0)
    m2 = next_iterate(m1)
    t = times(m0, m1)
    pair = m0 + m1
    total = times(5.0 * pair - t, m2) + 5.0 * t - 25.0 * (pair + m2)
    n = stat.shape[0]
    on_diagonal = lax.broadcasted_iota(jnp.int32, (n, n), 0) == lax.broadcasted_iota(
        jnp.int32, (n, n), 1
    )
    total = total + jnp.where(on_diagonal, 125.0, 0.0)
    return total * (lax.rsqrt(jnp.sqrt(c)) * (1.0 / 64.0))


def roots_kernel(owner_ref, refresh_ref, slot_ref, stat_ref, root_ref, out_ref):
    slot = slot_ref[0]

    def look(i, found):
        return found | jnp.where(owner_ref[refresh_ref[i]] == slot, 1, 0)

    fresh = lax.fori_loop(0, refresh_ref.shape[0], look, jnp.int32(0))

    @pl.when(fresh == 1)
    def _():
        out_ref[...] = root_of(stat_ref[...])

    @pl.when(fresh == 0)
    def _():
        out_ref[...] = root_ref[...]


def roots(owner_of, refresh, slot, stat, root):
    vmem = pl.BlockSpec(memory_space=pltpu.VMEM)
    smem = pl.BlockSpec(memory_space=pltpu.SMEM)
    return pl.pallas_call(
        roots_kernel,
        out_shape=jax.ShapeDtypeStruct(stat.shape, stat.dtype),
        in_specs=[smem, smem, smem, vmem, vmem],
        out_specs=vmem,
        compiler_params=pltpu.CompilerParams(vmem_limit_bytes=32 * MIB),
        cost_estimate=pl.CostEstimate(flops=8 * 2 * 512**3, bytes_accessed=3 * MIB, transcendentals=0),
    )(owner_of, refresh, slot, stat, root)


def finish_kernel(sources, n_owner, slot_ref, ls_ref, rs_ref, lr_ref, rr_ref, *refs):
    pieces, (up_ref, nl_ref, nr_ref, grad_ref) = refs[:-4], refs[-4:]
    owner = lax.rem(slot_ref[0], n_owner)
    z, y_hi, core = owner // 4, lax.rem(owner // 2, 2), lax.rem(owner, 2)
    n_z = n_owner // 4
    rows = pieces[0].shape[1]
    for piece, units in zip(pieces, sources):
        for i, (rz, yb, rc) in enumerate(units):
            z_from = lax.rem(z + (n_z - rz), n_z)
            y_from = 1 - y_hi if yb else y_hi
            core_from = 1 - core if rc else core
            row = pl.multiple_of((4 * z_from + 2 * y_from + core_from) * rows, rows)
            grad_ref[pl.ds(row, rows), :] = piece[i]
    grad = grad_ref[...]
    coeff = SHARE / grad.shape[1]
    f32 = jnp.float32
    left_part = jnp.dot(lr_ref[...].astype(jnp.bfloat16), grad, preferred_element_type=f32)
    up_ref[...] = jnp.dot(
        left_part.astype(jnp.bfloat16),
        rr_ref[...].astype(jnp.bfloat16),
        preferred_element_type=f32,
    ).astype(jnp.bfloat16)
    gram = lax.dot_general(grad, grad, (((1,), (1,)), ((), ())), preferred_element_type=f32)
    nl_ref[...] = DECAY * ls_ref[...] + coeff * gram
    gram = lax.dot_general(grad, grad, (((0,), (0,)), ((), ())), preferred_element_type=f32)
    nr_ref[...] = DECAY * rs_ref[...] + coeff * gram


def finish(slot, n_owner, pieces, sources, left_stat, right_stat, left_root, right_root):
    vmem = pl.BlockSpec(memory_space=pltpu.VMEM)
    smem = pl.BlockSpec(memory_space=pltpu.SMEM)
    return pl.pallas_call(
        functools.partial(finish_kernel, sources, n_owner),
        out_shape=[
            jax.ShapeDtypeStruct(left_stat.shape, jnp.bfloat16),
            jax.ShapeDtypeStruct(left_stat.shape, jnp.float32),
            jax.ShapeDtypeStruct(right_stat.shape, jnp.float32),
        ],
        in_specs=[smem] + [vmem] * (4 + len(pieces)),
        out_specs=[vmem] * 3,
        scratch_shapes=[pltpu.VMEM(left_stat.shape, jnp.bfloat16)],
        compiler_params=pltpu.CompilerParams(vmem_limit_bytes=32 * MIB),
        cost_estimate=pl.CostEstimate(flops=4 * 2 * 512**3, bytes_accessed=7 * MIB, transcendentals=0),
    )(slot, left_stat, right_stat, left_root, right_root, *pieces)


def plus(a, b):
    return (a.astype(jnp.float32) + b.astype(jnp.float32)).astype(jnp.bfloat16)


def per_device(grad_parts, owner_of, refresh, left_stat, right_stat, left_root, right_root):
    n_owner = lax.axis_size("owner")
    n_slots = lax.axis_size("dp") * n_owner
    my_slot = lax.axis_index("dp") * n_owner + lax.axis_index("owner")
    shard_rows = grad_parts[0]
    spans, table = build_table(n_slots, n_owner)
    mine = lax.dynamic_index_in_dim(jnp.asarray(table), my_slot, 0, keepdims=False)
    index = index_pieces(owner_of, mine)

    def send(x, **how):
        return lax.ppermute(x, AXES, route(n_slots, n_owner, **how))

    def step(name, number, x):
        orders = STREAMS[name][1]
        return lax.ppermute(x, AXES, route_step(n_slots, n_owner, orders, number))

    def rest(name, arrived, kept):
        for number in (1, 2):
            h = arrived.shape[0] // 2
            out = plus(arrived[h:], kept[h:])
            kept = plus(arrived[:h], kept[:h])
            arrived = step(name, number, out)
        return plus(arrived, kept)

    out = pick(index, shard_rows, [[spans["far", 1]], [spans["farthest", 1]]])
    far_in = step("far", 0, out[0])
    farthest_in = step("farthest", 0, out[1])
    ahead = pick(index, shard_rows, [[spans[("near", rz), 1], spans[("near", rz), 0]] for rz in (1, 7)])
    ahead = [send(p, rz=rz) for p, rz in zip(ahead, (1, 7))]
    kept = pick(
        index, shard_rows, [[spans[n, 0]] for n in ("far", "farthest", "middle", "here")]
    )
    middle_out, = pick(index, shard_rows, [[spans["middle", 1]]], after=(far_in, farthest_in))
    middle_in = step("middle", 0, middle_out)
    far = rest("far", far_in, kept[0])
    farthest = rest("farthest", farthest_in, kept[1])
    here_out, = pick(index, shard_rows, [[spans["here", 1]]], after=(middle_in,))
    here_in = step("here", 0, here_out)
    shape = (2, 2, 2, 4) + shard_rows.shape[1:]
    ahead = jnp.concatenate([p.reshape(shape) for p in ahead], axis=3)
    ahead = ahead.reshape((2, -1) + shard_rows.shape[1:])
    near_in = step("near", 0, ahead[0])
    middle = rest("middle", middle_in, kept[2])
    here = rest("here", here_in, kept[3])
    near = rest("near", near_in, ahead[1])

    travelled = [
        (3, send(far[:4], rz=3)),
        (5, send(far[4:], rz=5)),
        (4, send(farthest, rz=4)),
        (2, send(middle[:4], rz=2)),
        (6, send(middle[4:], rz=6)),
    ]
    at_home = [(0, here), (1, near[:4]), (7, near[4:])]
    pieces, sources = [], []
    for group in (travelled, at_home):
        for n, (yb, rc) in enumerate(QUAD):
            if (yb, rc) == (0, 0):
                for rz, x in group:
                    pieces.append(x[:1])
                    sources.append([(rz, yb, rc)])
                continue
            x = jnp.concatenate([x[n : n + 1] for _, x in group], axis=0)
            pieces.append(send(x, yb=yb, rc=rc))
            sources.append([(rz, yb, rc) for rz, _ in group])

    slot = my_slot.reshape(1)
    new_left_root = roots(owner_of, refresh, slot, left_stat[0], left_root[0])
    new_right_root = roots(owner_of, refresh, slot, right_stat[0], right_root[0])
    update, new_left, new_right = finish(
        slot, n_owner, pieces, sources, left_stat[0], right_stat[0], left_root[0], right_root[0]
    )
    return (
        update[None],
        new_left[None],
        new_right[None],
        new_left_root[None],
        new_right_root[None],
    )


def solution(mesh):
    owned = P(AXES, None, None)
    return jax.shard_map(
        per_device,
        mesh=mesh,
        in_specs=(P("dp", None, "owner", None), P(), P(), owned, owned, owned, owned),
        out_specs=(owned,) * 5,
        check_vma=False,
    )
```

```python
import functools

import jax
import jax.numpy as jnp
import numpy as np
from jax import lax
from jax.experimental import pallas as pl
from jax.experimental.pallas import tpu as pltpu
from jax.sharding import PartitionSpec as P

DECAY = 0.9
SHARE = 0.1
AXES = ("dp", "owner")
MIB = 1 << 20
CHUNKS = 8
MOST_MIB = 61

WIDE, SLIM = {0: "ayb", 1: "bay"}, {0: "yba", 1: "yba"}
X_OF, Y_OF = {"a": 1, "b": 3, "y": 0}, {"a": 0, "b": 0, "y": 1}


def build_streams(n_owner):
    cut = -(-2 * n_owner // 3)
    return [(0, cut, WIDE), (cut, n_owner - cut, SLIM)]


def route(n_slots, n_owner, orders, step):
    pairs = []
    for s in range(n_slots):
        data, owner = divmod(s, n_owner)
        dim = orders[owner % 2][step]
        to = (data // 2 ^ X_OF[dim]) * 2 + (data % 2 ^ Y_OF[dim])
        pairs.append((s, to * n_owner + owner))
    return pairs


def pick_kernel(groups, n_owner, chunks, n_after, slot_ref, owner_ref, shard_ref, *refs):
    outs, token = refs[n_after : n_after + len(groups)], refs[n_after + len(groups)]
    block_at, owners, sem = refs[n_after + len(groups) + 1 :][:3]
    copies = []
    if chunks:
        held, sems = refs[-2:]
        n = shard_ref.shape[0] // chunks
        for k in range(chunks):
            part = pl.ds(k * n, n)
            copies.append(pltpu.make_async_copy(shard_ref.at[part], held.at[part], sems.at[k]))
    else:
        held = shard_ref
    read_owners = pltpu.make_async_copy(owner_ref, owners, sem)
    read_owners.start()
    for copy in copies:
        copy.start()
    token[...] = jnp.zeros_like(token)
    slot = slot_ref[0]
    data, core = slot // n_owner, lax.rem(slot, 2)
    x, y_lo = data // 2, lax.rem(data, 2)
    read_owners.wait()

    @pl.loop(0, owners.shape[0], unroll=8)
    def _(b):
        block_at[owners[b]] = b

    for copy in copies:
        copy.wait()
    for out, (begin, count, orders, first) in zip(outs, groups):
        for second in (0, 1):
            for third in (0, 1):
                bits = (first, second, third)
                on_x, on_y = [0, 0], [0, 0]
                for c in (0, 1):
                    for dim, bit in zip(orders[c], (first, second, third)):
                        on_x[c] ^= X_OF[dim] * bit
                        on_y[c] ^= Y_OF[dim] * bit
                to_x = x ^ jnp.where(core == 0, on_x[0], on_x[1])
                to_y = y_lo ^ jnp.where(core == 0, on_y[0], on_y[1])
                base = (to_x * 2 + to_y) * n_owner + begin
                offset = (2 * second + third) * count

                @pl.loop(0, count, unroll=max(d for d in range(1, 12) if count % d == 0))
                def _(i, out=out, offset=offset, base=base):
                    out[offset + i] = held[block_at[base + i]]


def pick(slot, n_owner, owner_of, shard_rows, groups, after=(), chunks=0):
    _, rows, width = shard_rows.shape
    vmem = pl.BlockSpec(memory_space=pltpu.VMEM)
    smem = pl.BlockSpec(memory_space=pltpu.SMEM)
    anywhere = pl.BlockSpec(memory_space=pl.ANY)
    scratch = [
        pltpu.SMEM(owner_of.shape, jnp.int32),
        pltpu.SMEM(owner_of.shape, jnp.int32),
        pltpu.SemaphoreType.DMA,
    ]
    if chunks:
        scratch += [
            pltpu.VMEM(shard_rows.shape, shard_rows.dtype),
            pltpu.SemaphoreType.DMA((chunks,)),
        ]
    return pl.pallas_call(
        functools.partial(pick_kernel, groups, n_owner, chunks, len(after)),
        out_shape=[
            jax.ShapeDtypeStruct((4 * count, rows, width), shard_rows.dtype)
            for _, count, _, _ in groups
        ]
        + [jax.ShapeDtypeStruct((8, 128), jnp.float32)],
        in_specs=[smem, anywhere, anywhere if chunks else vmem] + [anywhere] * len(after),
        out_specs=[vmem] * (len(groups) + 1),
        scratch_shapes=scratch,
        compiler_params=pltpu.CompilerParams(vmem_limit_bytes=(MOST_MIB if chunks else 16) * MIB),
        cost_estimate=pl.CostEstimate(flops=0, bytes_accessed=1024, transcendentals=0),
    )(slot, owner_of, shard_rows, *after)


def event_kernel(plan, n_in, n_after, *refs):
    ins, outs = refs[:n_in], refs[n_in + n_after :]
    for out, parts in zip(outs, plan):
        offset = 0
        for count, sources in parts:

            @pl.loop(0, count, unroll=max(d for d in range(1, 12) if count % d == 0))
            def _(i, out=out, offset=offset, sources=sources):
                total = [ins[ref][start + i].astype(jnp.float32) for ref, start in sources]
                out[offset + i] = sum(total[1:], total[0]).astype(out.dtype)

            offset += count


def event(arrays, plan, after):
    piece = arrays[0].shape[1:]
    vmem = pl.BlockSpec(memory_space=pltpu.VMEM)
    counts = [sum(n for n, _ in parts) for parts in plan]
    return pl.pallas_call(
        functools.partial(event_kernel, plan, len(arrays), len(after)),
        out_shape=[jax.ShapeDtypeStruct((n,) + piece, arrays[0].dtype) for n in counts],
        in_specs=[vmem] * len(arrays) + [pl.BlockSpec(memory_space=pl.ANY)] * len(after),
        out_specs=[vmem] * len(counts),
        compiler_params=pltpu.CompilerParams(vmem_limit_bytes=16 * MIB),
        cost_estimate=pl.CostEstimate(flops=0, bytes_accessed=1024, transcendentals=0),
    )(*arrays, *after)


def times(a, b):
    return jnp.dot(
        a.astype(jnp.bfloat16), b.astype(jnp.bfloat16), preferred_element_type=jnp.float32
    )


def next_iterate(m):
    d = (times(m, m) - 10.0 * m) * (1.0 / 16.0)
    e = times(d, d) + 3.125 * d
    return (625.0 / 256.0) * m + times(e, m)


def root_of(stat):
    c = jnp.sqrt(jnp.sum(stat * stat))
    m0 = stat / c
    m1 = next_iterate(m0)
    m2 = next_iterate(m1)
    t = times(m0, m1)
    pair = m0 + m1
    total = times(5.0 * pair - t, m2) + 5.0 * t - 25.0 * (pair + m2)
    n = stat.shape[0]
    on_diagonal = lax.broadcasted_iota(jnp.int32, (n, n), 0) == lax.broadcasted_iota(
        jnp.int32, (n, n), 1
    )
    total = total + jnp.where(on_diagonal, 125.0, 0.0)
    return total * (lax.rsqrt(jnp.sqrt(c)) * (1.0 / 64.0))


def roots_kernel(owner_ref, refresh_ref, slot_ref, ls_ref, rs_ref, lr_ref, rr_ref, _, left_ref, right_ref, token_ref):
    token_ref[...] = jnp.zeros_like(token_ref)
    slot = slot_ref[0]

    def look(i, found):
        return found | jnp.where(owner_ref[refresh_ref[i]] == slot, 1, 0)

    fresh = lax.fori_loop(0, refresh_ref.shape[0], look, jnp.int32(0))

    @pl.when(fresh == 1)
    def _():
        left_ref[...] = root_of(ls_ref[...])
        right_ref[...] = root_of(rs_ref[...])

    @pl.when(fresh == 0)
    def _():
        left_ref[...] = lr_ref[...]
        right_ref[...] = rr_ref[...]


def roots(owner_of, refresh, slot, stats_and_roots, after):
    vmem = pl.BlockSpec(memory_space=pltpu.VMEM)
    smem = pl.BlockSpec(memory_space=pltpu.SMEM)
    stat = stats_and_roots[0]
    return pl.pallas_call(
        roots_kernel,
        out_shape=[jax.ShapeDtypeStruct(stat.shape, stat.dtype)] * 2
        + [jax.ShapeDtypeStruct((8, 128), jnp.float32)],
        in_specs=[smem] * 3 + [vmem] * 4 + [pl.BlockSpec(memory_space=pl.ANY)],
        out_specs=[vmem] * 3,
        compiler_params=pltpu.CompilerParams(vmem_limit_bytes=32 * MIB),
        cost_estimate=pl.CostEstimate(flops=0, bytes_accessed=1024, transcendentals=0),
    )(owner_of, refresh, slot, *stats_and_roots, after)


def finish_kernel(grad_ref, ls_ref, rs_ref, lr_ref, rr_ref, up_out, nl_out, nr_out, up_ref, nl_ref, nr_ref, sems):
    writes = [
        pltpu.make_async_copy(src, dst, sems.at[k])
        for k, (src, dst) in enumerate(((up_ref, up_out), (nl_ref, nl_out), (nr_ref, nr_out)))
    ]
    grad = grad_ref[...]
    coeff = SHARE / grad.shape[1]
    f32 = jnp.float32
    gram = lax.dot_general(grad, grad, (((1,), (1,)), ((), ())), preferred_element_type=f32)
    nl_ref[...] = DECAY * ls_ref[...] + coeff * gram
    writes[1].start()
    gram = lax.dot_general(grad, grad, (((0,), (0,)), ((), ())), preferred_element_type=f32)
    nr_ref[...] = DECAY * rs_ref[...] + coeff * gram
    writes[2].start()
    left_part = jnp.dot(lr_ref[...].astype(jnp.bfloat16), grad, preferred_element_type=f32)
    up_ref[...] = jnp.dot(
        left_part.astype(jnp.bfloat16),
        rr_ref[...].astype(jnp.bfloat16),
        preferred_element_type=f32,
    ).astype(jnp.bfloat16)
    writes[0].start()
    for write in writes:
        write.wait()


def finish(grad, left_stat, right_stat, left_root, right_root):
    vmem = pl.BlockSpec(memory_space=pltpu.VMEM)
    out_shape = [
        jax.ShapeDtypeStruct(grad.shape, jnp.bfloat16),
        jax.ShapeDtypeStruct(left_stat.shape, jnp.float32),
        jax.ShapeDtypeStruct(right_stat.shape, jnp.float32),
    ]
    return pl.pallas_call(
        finish_kernel,
        out_shape=out_shape,
        in_specs=[vmem] * 5,
        out_specs=[pl.BlockSpec(memory_space=pl.ANY)] * 3,
        scratch_shapes=[pltpu.VMEM(x.shape, x.dtype) for x in out_shape]
        + [pltpu.SemaphoreType.DMA((3,))],
        compiler_params=pltpu.CompilerParams(vmem_limit_bytes=16 * MIB),
        cost_estimate=pl.CostEstimate(flops=4 * 2 * 512**3, bytes_accessed=7 * MIB, transcendentals=0),
    )(grad, left_stat, right_stat, left_root, right_root)


def per_device(grad_parts, owner_of, refresh, left_stat, right_stat, left_root, right_root):
    n_owner = lax.axis_size("owner")
    n_slots = lax.axis_size("dp") * n_owner
    slot = (lax.axis_index("dp") * n_owner + lax.axis_index("owner")).reshape(1)
    shard_rows = grad_parts[0]
    streams = build_streams(n_owner)
    def step(stream, number, x):
        return lax.ppermute(x, AXES, route(n_slots, n_owner, stream[2], number))

    def groups(first):
        return [stream + (first,) for stream in streams]

    def steps(number, sent):
        return [step(stream, number, x) for stream, x in zip(streams, sent)]

    def add(number, got, kept, token):
        arrays = [x for pair in zip(got, kept) for x in pair]
        halves = [count * (2 if number == 1 else 1) for _, count, _ in streams]

        def part(second):
            return [
                [(half, [(2 * k, second * half), (2 * k + 1, second * half)])]
                for k, half in enumerate(halves)
            ]

        sent = event(arrays, part(1), (token,))
        kept = event(arrays, part(0), (sent[0],))
        return sent, kept, kept[0]

    def total(got, kept, token):
        arrays = [x for pair in zip(got, kept) for x in pair]
        parts = [(count, [(2 * k, 0), (2 * k + 1, 0)]) for k, (_, count, _) in enumerate(streams)]
        return event(arrays, [parts], (token,))[0]

    def to_owners(x):
        x = lax.all_to_all(x, "owner", split_axis=0, concat_axis=0, tiled=True)
        return x.reshape(-1, x.shape[2])

    *sent, token = pick(slot, n_owner, owner_of, shard_rows, groups(1), chunks=CHUNKS)
    got = steps(0, sent)
    *kept, token = pick(slot, n_owner, owner_of, shard_rows, groups(0), (token,))
    stats_and_roots = [x[0] for x in (left_stat, right_stat, left_root, right_root)]
    new_left_root, new_right_root, token = roots(
        owner_of, refresh, slot, stats_and_roots, token
    )
    for number in (1, 2):
        sent, kept, token = add(number, got, kept, token)
        got = steps(number, sent)
    grad = total(got, kept, token)
    update, new_left, new_right = finish(to_owners(grad), *stats_and_roots)
    return (
        update[None],
        new_left[None],
        new_right[None],
        new_left_root[None],
        new_right_root[None],
    )


def solution(mesh):
    owned = P(AXES, None, None)
    return jax.shard_map(
        per_device,
        mesh=mesh,
        in_specs=(P("dp", None, "owner", None), P(), P(), owned, owned, owned, owned),
        out_specs=(owned,) * 5,
        check_vma=False,
    )
```

```python
import functools

import jax
import jax.numpy as jnp
import numpy as np
from jax import lax
from jax.experimental import pallas as pl
from jax.experimental.pallas import tpu as pltpu
from jax.sharding import PartitionSpec as P

DECAY = 0.9
SHARE = 0.1
AXES = ("dp", "owner")
MIB = 1 << 20
CHUNKS = 8
MOST_MIB = 61

WIDE, SLIM = {0: "ayb", 1: "bay"}, {0: "yba", 1: "yba"}
X_OF, Y_OF = {"a": 1, "b": 3, "y": 0}, {"a": 0, "b": 0, "y": 1}


def build_streams(n_places):
    cut = -(-2 * n_places // 3)
    return [(0, cut, WIDE), (cut, n_places - cut, SLIM)]


def route(n_slots, n_owner, orders, step, other=0):
    pairs = []
    for s in range(n_slots):
        data, owner = divmod(s, n_owner)
        if orders is not None:
            dim = orders[owner % 2 ^ other][step]
            data = (data // 2 ^ X_OF[dim]) * 2 + (data % 2 ^ Y_OF[dim])
        pairs.append((s, data * n_owner + (owner ^ other)))
    return pairs


def pick_kernel(plan, n_owner, chunks, n_after, slot_ref, owner_ref, shard_ref, *refs):
    outs, token = refs[n_after : n_after + len(plan)], refs[n_after + len(plan)]
    block_at, owners, sem = refs[n_after + len(plan) + 1 :][:3]
    copies = []
    if chunks:
        held, sems = refs[-2:]
        n = shard_ref.shape[0] // chunks
        for k in range(chunks):
            part = pl.ds(k * n, n)
            copies.append(pltpu.make_async_copy(shard_ref.at[part], held.at[part], sems.at[k]))
    else:
        held = shard_ref
    read_owners = pltpu.make_async_copy(owner_ref, owners, sem)
    read_owners.start()
    for copy in copies:
        copy.start()
    token[...] = jnp.zeros_like(token)
    slot = slot_ref[0]
    data, my_core = slot // n_owner, lax.rem(slot, 2)
    x, y_lo = data // 2, lax.rem(data, 2)
    read_owners.wait()

    @pl.loop(0, owners.shape[0], unroll=8)
    def _(b):
        block_at[owners[b]] = b

    for copy in copies:
        copy.wait()
    for out, groups in zip(outs, plan):
        offset = 0
        for begin, count, orders, first, other in groups:
            core = 1 - my_core if other else my_core
            for second in (0, 1):
                for third in (0, 1):
                    on_x, on_y = [0, 0], [0, 0]
                    for c in (0, 1):
                        for dim, bit in zip(orders[c], (first, second, third)):
                            on_x[c] ^= X_OF[dim] * bit
                            on_y[c] ^= Y_OF[dim] * bit
                    to_x = x ^ jnp.where(core == 0, on_x[0], on_x[1])
                    to_y = y_lo ^ jnp.where(core == 0, on_y[0], on_y[1])
                    base = (to_x * 2 + to_y) * n_owner + 2 * begin + core

                    @pl.loop(0, count, unroll=count)
                    def _(i, out=out, offset=offset, base=base):
                        out[offset + i] = held[block_at[base + 2 * i]]

                    offset += count


def pick(slot, n_owner, owner_of, shard_rows, plan, after=(), chunks=0):
    _, rows, width = shard_rows.shape
    vmem = pl.BlockSpec(memory_space=pltpu.VMEM)
    smem = pl.BlockSpec(memory_space=pltpu.SMEM)
    anywhere = pl.BlockSpec(memory_space=pl.ANY)
    scratch = [
        pltpu.SMEM(owner_of.shape, jnp.int32),
        pltpu.SMEM(owner_of.shape, jnp.int32),
        pltpu.SemaphoreType.DMA,
    ]
    if chunks:
        scratch += [
            pltpu.VMEM(shard_rows.shape, shard_rows.dtype),
            pltpu.SemaphoreType.DMA((chunks,)),
        ]
    return pl.pallas_call(
        functools.partial(pick_kernel, plan, n_owner, chunks, len(after)),
        out_shape=[
            jax.ShapeDtypeStruct((4 * sum(g[1] for g in groups), rows, width), shard_rows.dtype)
            for groups in plan
        ]
        + [jax.ShapeDtypeStruct((8, 128), jnp.float32)],
        in_specs=[smem, anywhere, anywhere if chunks else vmem] + [anywhere] * len(after),
        out_specs=[vmem] * (len(plan) + 1),
        scratch_shapes=scratch,
        compiler_params=pltpu.CompilerParams(vmem_limit_bytes=(MOST_MIB if chunks else 16) * MIB),
        cost_estimate=pl.CostEstimate(flops=0, bytes_accessed=1024, transcendentals=0),
    )(slot, owner_of, shard_rows, *after)


def first_sum_kernel(counts, second, slot_ref, handed_ref, *refs):
    n = len(counts)
    core = lax.rem(slot_ref[0], 2)
    offset = 0
    for k, count in enumerate(counts):
        same, other, own, out = refs[3 * k], refs[3 * k + 1], refs[3 * k + 2], refs[3 * n + 1 + k]

        @pl.loop(0, 2 * count, unroll=count)
        def _(i, same=same, other=other, own=own, out=out, offset=offset, count=count):
            j = 2 * count * second + i
            f32 = jnp.float32
            out[2 * i + core] = (same[j].astype(f32) + own[j].astype(f32)).astype(out.dtype)
            out[2 * i + 1 - core] = (
                other[j].astype(f32) + handed_ref[offset + j].astype(f32)
            ).astype(out.dtype)

        offset += 4 * count


def first_sum(slot, counts, second, handed, arrays, after):
    vmem = pl.BlockSpec(memory_space=pltpu.VMEM)
    return pl.pallas_call(
        functools.partial(first_sum_kernel, counts, second),
        out_shape=[
            jax.ShapeDtypeStruct((4 * count,) + handed.shape[1:], handed.dtype) for count in counts
        ],
        in_specs=[pl.BlockSpec(memory_space=pltpu.SMEM)]
        + [vmem] * (1 + len(arrays))
        + [pl.BlockSpec(memory_space=pl.ANY)],
        out_specs=[vmem] * len(counts),
        compiler_params=pltpu.CompilerParams(vmem_limit_bytes=16 * MIB),
        cost_estimate=pl.CostEstimate(flops=0, bytes_accessed=1024, transcendentals=0),
    )(slot, handed, *arrays, after)


def event_kernel(plan, n_in, n_after, *refs):
    ins, outs = refs[:n_in], refs[n_in + n_after :]
    for out, parts in zip(outs, plan):
        offset = 0
        for count, sources in parts:

            @pl.loop(0, count, unroll=max(d for d in range(1, 12) if count % d == 0))
            def _(i, out=out, offset=offset, sources=sources):
                total = [ins[ref][start + i].astype(jnp.float32) for ref, start in sources]
                out[offset + i] = sum(total[1:], total[0]).astype(out.dtype)

            offset += count


def event(arrays, plan, after):
    piece = arrays[0].shape[1:]
    vmem = pl.BlockSpec(memory_space=pltpu.VMEM)
    counts = [sum(n for n, _ in parts) for parts in plan]
    return pl.pallas_call(
        functools.partial(event_kernel, plan, len(arrays), len(after)),
        out_shape=[jax.ShapeDtypeStruct((n,) + piece, arrays[0].dtype) for n in counts],
        in_specs=[vmem] * len(arrays) + [pl.BlockSpec(memory_space=pl.ANY)] * len(after),
        out_specs=[vmem] * len(counts),
        compiler_params=pltpu.CompilerParams(vmem_limit_bytes=16 * MIB),
        cost_estimate=pl.CostEstimate(flops=0, bytes_accessed=1024, transcendentals=0),
    )(*arrays, *after)


def times(a, b):
    return jnp.dot(
        a.astype(jnp.bfloat16), b.astype(jnp.bfloat16), preferred_element_type=jnp.float32
    )


def next_iterate(m):
    d = (times(m, m) - 10.0 * m) * (1.0 / 16.0)
    e = times(d, d) + 3.125 * d
    return (625.0 / 256.0) * m + times(e, m)


def root_of(stat):
    c = jnp.sqrt(jnp.sum(stat * stat))
    m0 = stat / c
    m1 = next_iterate(m0)
    m2 = next_iterate(m1)
    t = times(m0, m1)
    pair = m0 + m1
    total = times(5.0 * pair - t, m2) + 5.0 * t - 25.0 * (pair + m2)
    n = stat.shape[0]
    on_diagonal = lax.broadcasted_iota(jnp.int32, (n, n), 0) == lax.broadcasted_iota(
        jnp.int32, (n, n), 1
    )
    total = total + jnp.where(on_diagonal, 125.0, 0.0)
    return total * (lax.rsqrt(jnp.sqrt(c)) * (1.0 / 64.0))


def roots_kernel(owner_ref, refresh_ref, slot_ref, ls_ref, rs_ref, lr_ref, rr_ref, _, left_ref, right_ref, token_ref):
    token_ref[...] = jnp.zeros_like(token_ref)
    slot = slot_ref[0]

    def look(i, found):
        return found | jnp.where(owner_ref[refresh_ref[i]] == slot, 1, 0)

    fresh = lax.fori_loop(0, refresh_ref.shape[0], look, jnp.int32(0))

    @pl.when(fresh == 1)
    def _():
        left_ref[...] = root_of(ls_ref[...])
        right_ref[...] = root_of(rs_ref[...])

    @pl.when(fresh == 0)
    def _():
        left_ref[...] = lr_ref[...]
        right_ref[...] = rr_ref[...]


def roots(owner_of, refresh, slot, stats_and_roots, after):
    vmem = pl.BlockSpec(memory_space=pltpu.VMEM)
    smem = pl.BlockSpec(memory_space=pltpu.SMEM)
    stat = stats_and_roots[0]
    return pl.pallas_call(
        roots_kernel,
        out_shape=[jax.ShapeDtypeStruct(stat.shape, stat.dtype)] * 2
        + [jax.ShapeDtypeStruct((8, 128), jnp.float32)],
        in_specs=[smem] * 3 + [vmem] * 4 + [pl.BlockSpec(memory_space=pl.ANY)],
        out_specs=[vmem] * 3,
        compiler_params=pltpu.CompilerParams(vmem_limit_bytes=32 * MIB),
        cost_estimate=pl.CostEstimate(flops=0, bytes_accessed=1024, transcendentals=0),
    )(owner_of, refresh, slot, *stats_and_roots, after)


def finish_kernel(grad_ref, ls_ref, rs_ref, lr_ref, rr_ref, up_out, nl_out, nr_out, up_ref, nl_ref, nr_ref, sems):
    writes = [
        pltpu.make_async_copy(src, dst, sems.at[k])
        for k, (src, dst) in enumerate(((up_ref, up_out), (nl_ref, nl_out), (nr_ref, nr_out)))
    ]
    grad = grad_ref[...]
    coeff = SHARE / grad.shape[1]
    f32 = jnp.float32
    gram = lax.dot_general(grad, grad, (((1,), (1,)), ((), ())), preferred_element_type=f32)
    nl_ref[...] = DECAY * ls_ref[...] + coeff * gram
    writes[1].start()
    gram = lax.dot_general(grad, grad, (((0,), (0,)), ((), ())), preferred_element_type=f32)
    nr_ref[...] = DECAY * rs_ref[...] + coeff * gram
    writes[2].start()
    left_part = jnp.dot(lr_ref[...].astype(jnp.bfloat16), grad, preferred_element_type=f32)
    up_ref[...] = jnp.dot(
        left_part.astype(jnp.bfloat16),
        rr_ref[...].astype(jnp.bfloat16),
        preferred_element_type=f32,
    ).astype(jnp.bfloat16)
    writes[0].start()
    for write in writes:
        write.wait()


def finish(grad, left_stat, right_stat, left_root, right_root):
    vmem = pl.BlockSpec(memory_space=pltpu.VMEM)
    out_shape = [
        jax.ShapeDtypeStruct(grad.shape, jnp.bfloat16),
        jax.ShapeDtypeStruct(left_stat.shape, jnp.float32),
        jax.ShapeDtypeStruct(right_stat.shape, jnp.float32),
    ]
    return pl.pallas_call(
        finish_kernel,
        out_shape=out_shape,
        in_specs=[vmem] * 5,
        out_specs=[pl.BlockSpec(memory_space=pl.ANY)] * 3,
        scratch_shapes=[pltpu.VMEM(x.shape, x.dtype) for x in out_shape]
        + [pltpu.SemaphoreType.DMA((3,))],
        compiler_params=pltpu.CompilerParams(vmem_limit_bytes=16 * MIB),
        cost_estimate=pl.CostEstimate(flops=4 * 2 * 512**3, bytes_accessed=7 * MIB, transcendentals=0),
    )(grad, left_stat, right_stat, left_root, right_root)


def per_device(grad_parts, owner_of, refresh, left_stat, right_stat, left_root, right_root):
    n_owner = lax.axis_size("owner")
    n_slots = lax.axis_size("dp") * n_owner
    slot = (lax.axis_index("dp") * n_owner + lax.axis_index("owner")).reshape(1)
    shard_rows = grad_parts[0]
    streams = build_streams(n_owner // 2)
    counts = [2 * count for _, count, _ in streams]

    def send(x, *how):
        return lax.ppermute(x, AXES, route(n_slots, n_owner, *how))

    def steps(number, sent, other=0):
        return [send(x, orders, number, other) for (_, _, orders), x in zip(streams, sent)]

    def total(got, kept, token):
        arrays = [x for pair in zip(got, kept) for x in pair]
        parts = [(count, [(2 * k, 0), (2 * k + 1, 0)]) for k, count in enumerate(counts)]
        return event(arrays, [parts], (token,))[0]

    def to_owners(x):
        groups = [list(range(core, n_owner, 2)) for core in (0, 1)]
        x = x.reshape(n_owner // 2, -1, x.shape[2])
        x = lax.all_to_all(
            x, "owner", split_axis=0, concat_axis=0, tiled=True, axis_index_groups=groups
        )
        return x.reshape(-1, x.shape[2])

    plan = [[stream + (0, 1) for stream in streams]]
    plan += [[stream + (1, other)] for other in (0, 1) for stream in streams]
    handed, *sent, token = pick(slot, n_owner, owner_of, shard_rows, plan, chunks=CHUNKS)
    handed = send(handed, None, 0, 1)
    same, other = steps(0, sent[: len(streams)]), steps(0, sent[len(streams) :], 1)
    plan = [[stream + (0, 0)] for stream in streams]
    *own, token = pick(slot, n_owner, owner_of, shard_rows, plan, (token,))
    stats_and_roots = [x[0] for x in (left_stat, right_stat, left_root, right_root)]
    new_left_root, new_right_root, token = roots(
        owner_of, refresh, slot, stats_and_roots, token
    )
    places = [count for _, count, _ in streams]
    arrays = [x for three in zip(same, other, own) for x in three]
    sent = first_sum(slot, places, 1, handed, arrays, token)
    got = steps(1, sent)
    kept = first_sum(slot, places, 0, handed, arrays, sent[0])

    def part(second):
        return [
            [(count, [(2 * k, second * count), (2 * k + 1, second * count)])]
            for k, count in enumerate(counts)
        ]

    arrays = [x for pair in zip(got, kept) for x in pair]
    sent = event(arrays, part(1), (kept[0],))
    got = steps(2, sent)
    kept = event(arrays, part(0), (sent[0],))
    token = kept[0]
    grad = total(got, kept, token)
    update, new_left, new_right = finish(to_owners(grad), *stats_and_roots)
    return (
        update[None],
        new_left[None],
        new_right[None],
        new_left_root[None],
        new_right_root[None],
    )


def solution(mesh):
    owned = P(AXES, None, None)
    return jax.shard_map(
        per_device,
        mesh=mesh,
        in_specs=(P("dp", None, "owner", None), P(), P(), owned, owned, owned, owned),
        out_specs=(owned,) * 5,
        check_vma=False,
    )
```

```python
import functools

import jax
import jax.numpy as jnp
import numpy as np
from jax import lax
from jax.experimental import pallas as pl
from jax.experimental.pallas import tpu as pltpu
from jax.sharding import PartitionSpec as P

DECAY = 0.9
SHARE = 0.1
AXES = ("dp", "owner")
MIB = 1 << 20
CHUNKS = 8
MOST_MIB = 61

WIDE, SLIM = {0: "ayb", 1: "bay"}, {0: "yba", 1: "yba"}
X_OF, Y_OF = {"a": 1, "b": 3, "y": 0}, {"a": 0, "b": 0, "y": 1}


def build_streams(n_places):
    cut = -(-2 * n_places // 3)
    return [(0, cut, WIDE), (cut, n_places - cut, SLIM)]


def route(n_slots, n_owner, orders, step, other=0):
    pairs = []
    for s in range(n_slots):
        data, owner = divmod(s, n_owner)
        if orders is not None:
            dim = orders[owner % 2 ^ other][step]
            data = (data // 2 ^ X_OF[dim]) * 2 + (data % 2 ^ Y_OF[dim])
        pairs.append((s, data * n_owner + (owner ^ other)))
    return pairs


def pick_kernel(plan, n_owner, chunks, n_after, slot_ref, owner_ref, shard_ref, *refs):
    outs, token = refs[n_after : n_after + len(plan)], refs[n_after + len(plan)]
    block_at, owners, sem = refs[n_after + len(plan) + 1 :][:3]
    copies = []
    if chunks:
        held, sems = refs[-2:]
        n = shard_ref.shape[0] // chunks
        for k in range(chunks):
            part = pl.ds(k * n, n)
            copies.append(pltpu.make_async_copy(shard_ref.at[part], held.at[part], sems.at[k]))
    else:
        held = shard_ref
    read_owners = pltpu.make_async_copy(owner_ref, owners, sem)
    read_owners.start()
    for copy in copies:
        copy.start()
    token[...] = jnp.zeros_like(token)
    slot = slot_ref[0]
    data, my_core = slot // n_owner, lax.rem(slot, 2)
    x, y_lo = data // 2, lax.rem(data, 2)
    read_owners.wait()

    @pl.loop(0, owners.shape[0], unroll=8)
    def _(b):
        block_at[owners[b]] = b

    for copy in copies:
        copy.wait()
    for out, groups in zip(outs, plan):
        offset = 0
        for begin, count, orders, first, other in groups:
            core = 1 - my_core if other else my_core
            for second in (0, 1):
                for third in (0, 1):
                    on_x, on_y = [0, 0], [0, 0]
                    for c in (0, 1):
                        for dim, bit in zip(orders[c], (first, second, third)):
                            on_x[c] ^= X_OF[dim] * bit
                            on_y[c] ^= Y_OF[dim] * bit
                    to_x = x ^ jnp.where(core == 0, on_x[0], on_x[1])
                    to_y = y_lo ^ jnp.where(core == 0, on_y[0], on_y[1])
                    base = (to_x * 2 + to_y) * n_owner + 2 * begin + core

                    @pl.loop(0, count, unroll=count)
                    def _(i, out=out, offset=offset, base=base):
                        out[offset + i] = held[block_at[base + 2 * i]]

                    offset += count


def pick(slot, n_owner, owner_of, shard_rows, plan, after=(), chunks=0):
    _, rows, width = shard_rows.shape
    vmem = pl.BlockSpec(memory_space=pltpu.VMEM)
    smem = pl.BlockSpec(memory_space=pltpu.SMEM)
    anywhere = pl.BlockSpec(memory_space=pl.ANY)
    scratch = [
        pltpu.SMEM(owner_of.shape, jnp.int32),
        pltpu.SMEM(owner_of.shape, jnp.int32),
        pltpu.SemaphoreType.DMA,
    ]
    if chunks:
        scratch += [
            pltpu.VMEM(shard_rows.shape, shard_rows.dtype),
            pltpu.SemaphoreType.DMA((chunks,)),
        ]
    return pl.pallas_call(
        functools.partial(pick_kernel, plan, n_owner, chunks, len(after)),
        out_shape=[
            jax.ShapeDtypeStruct((4 * sum(g[1] for g in groups), rows, width), shard_rows.dtype)
            for groups in plan
        ]
        + [jax.ShapeDtypeStruct((8, 128), jnp.float32)],
        in_specs=[smem, anywhere, anywhere if chunks else vmem] + [anywhere] * len(after),
        out_specs=[vmem] * (len(plan) + 1),
        scratch_shapes=scratch,
        compiler_params=pltpu.CompilerParams(vmem_limit_bytes=(MOST_MIB if chunks else 16) * MIB),
        cost_estimate=pl.CostEstimate(flops=0, bytes_accessed=1024, transcendentals=0),
    )(slot, owner_of, shard_rows, *after)


def first_sum_kernel(counts, second, slot_ref, handed_ref, *refs):
    n = len(counts)
    core = lax.rem(slot_ref[0], 2)
    offset = 0
    for k, count in enumerate(counts):
        same, other, out = refs[2 * k], refs[2 * k + 1], refs[2 * n + 1 + k]

        @pl.loop(0, 2 * count, unroll=count)
        def _(i, same=same, other=other, out=out, offset=offset, count=count):
            j = 2 * count * second + i
            f32 = jnp.float32
            out[2 * i + core] = same[j]
            out[2 * i + 1 - core] = (
                other[j].astype(f32) + handed_ref[offset + j].astype(f32)
            ).astype(out.dtype)

        offset += 4 * count


def first_sum(slot, counts, second, handed, arrays, after):
    vmem = pl.BlockSpec(memory_space=pltpu.VMEM)
    return pl.pallas_call(
        functools.partial(first_sum_kernel, counts, second),
        out_shape=[
            jax.ShapeDtypeStruct((4 * count,) + handed.shape[1:], handed.dtype) for count in counts
        ],
        in_specs=[pl.BlockSpec(memory_space=pltpu.SMEM)]
        + [vmem] * (1 + len(arrays))
        + [pl.BlockSpec(memory_space=pl.ANY)],
        out_specs=[vmem] * len(counts),
        compiler_params=pltpu.CompilerParams(vmem_limit_bytes=16 * MIB),
        cost_estimate=pl.CostEstimate(flops=0, bytes_accessed=1024, transcendentals=0),
    )(slot, handed, *arrays, after)


def event_kernel(plan, n_in, n_after, *refs):
    ins, outs = refs[:n_in], refs[n_in + n_after :]
    for out, parts in zip(outs, plan):
        offset = 0
        for count, sources in parts:

            @pl.loop(0, count, unroll=max(d for d in range(1, 12) if count % d == 0))
            def _(i, out=out, offset=offset, sources=sources):
                total = [ins[ref][start + i].astype(jnp.float32) for ref, start in sources]
                out[offset + i] = sum(total[1:], total[0]).astype(out.dtype)

            offset += count


def event(arrays, plan, after):
    piece = arrays[0].shape[1:]
    vmem = pl.BlockSpec(memory_space=pltpu.VMEM)
    counts = [sum(n for n, _ in parts) for parts in plan]
    return pl.pallas_call(
        functools.partial(event_kernel, plan, len(arrays), len(after)),
        out_shape=[jax.ShapeDtypeStruct((n,) + piece, arrays[0].dtype) for n in counts],
        in_specs=[vmem] * len(arrays) + [pl.BlockSpec(memory_space=pl.ANY)] * len(after),
        out_specs=[vmem] * len(counts),
        compiler_params=pltpu.CompilerParams(vmem_limit_bytes=16 * MIB),
        cost_estimate=pl.CostEstimate(flops=0, bytes_accessed=1024, transcendentals=0),
    )(*arrays, *after)


def times(a, b):
    return jnp.dot(
        a.astype(jnp.bfloat16), b.astype(jnp.bfloat16), preferred_element_type=jnp.float32
    )


def next_iterate(m):
    d = (times(m, m) - 10.0 * m) * (1.0 / 16.0)
    e = times(d, d) + 3.125 * d
    return (625.0 / 256.0) * m + times(e, m)


def root_of(stat):
    c = jnp.sqrt(jnp.sum(stat * stat))
    m0 = stat / c
    m1 = next_iterate(m0)
    m2 = next_iterate(m1)
    t = times(m0, m1)
    pair = m0 + m1
    total = times(5.0 * pair - t, m2) + 5.0 * t - 25.0 * (pair + m2)
    n = stat.shape[0]
    on_diagonal = lax.broadcasted_iota(jnp.int32, (n, n), 0) == lax.broadcasted_iota(
        jnp.int32, (n, n), 1
    )
    total = total + jnp.where(on_diagonal, 125.0, 0.0)
    return total * (lax.rsqrt(jnp.sqrt(c)) * (1.0 / 64.0))


def roots_kernel(owner_ref, refresh_ref, slot_ref, ls_ref, rs_ref, lr_ref, rr_ref, _, left_ref, right_ref, token_ref):
    token_ref[...] = jnp.zeros_like(token_ref)
    slot = slot_ref[0]

    def look(i, found):
        return found | jnp.where(owner_ref[refresh_ref[i]] == slot, 1, 0)

    fresh = lax.fori_loop(0, refresh_ref.shape[0], look, jnp.int32(0))

    @pl.when(fresh == 1)
    def _():
        left_ref[...] = root_of(ls_ref[...])
        right_ref[...] = root_of(rs_ref[...])

    @pl.when(fresh == 0)
    def _():
        left_ref[...] = lr_ref[...]
        right_ref[...] = rr_ref[...]


def roots(owner_of, refresh, slot, stats_and_roots, after):
    vmem = pl.BlockSpec(memory_space=pltpu.VMEM)
    smem = pl.BlockSpec(memory_space=pltpu.SMEM)
    stat = stats_and_roots[0]
    return pl.pallas_call(
        roots_kernel,
        out_shape=[jax.ShapeDtypeStruct(stat.shape, stat.dtype)] * 2
        + [jax.ShapeDtypeStruct((8, 128), jnp.float32)],
        in_specs=[smem] * 3 + [vmem] * 4 + [pl.BlockSpec(memory_space=pl.ANY)],
        out_specs=[vmem] * 3,
        compiler_params=pltpu.CompilerParams(vmem_limit_bytes=32 * MIB),
        cost_estimate=pl.CostEstimate(flops=0, bytes_accessed=1024, transcendentals=0),
    )(owner_of, refresh, slot, *stats_and_roots, after)


def finish_kernel(grad_ref, ls_ref, rs_ref, lr_ref, rr_ref, up_out, nl_out, nr_out, up_ref, nl_ref, nr_ref, sems):
    writes = [
        pltpu.make_async_copy(src, dst, sems.at[k])
        for k, (src, dst) in enumerate(((up_ref, up_out), (nl_ref, nl_out), (nr_ref, nr_out)))
    ]
    grad = grad_ref[...]
    coeff = SHARE / grad.shape[1]
    f32 = jnp.float32
    gram = lax.dot_general(grad, grad, (((1,), (1,)), ((), ())), preferred_element_type=f32)
    nl_ref[...] = DECAY * ls_ref[...] + coeff * gram
    writes[1].start()
    gram = lax.dot_general(grad, grad, (((0,), (0,)), ((), ())), preferred_element_type=f32)
    nr_ref[...] = DECAY * rs_ref[...] + coeff * gram
    writes[2].start()
    left_part = jnp.dot(lr_ref[...].astype(jnp.bfloat16), grad, preferred_element_type=f32)
    up_ref[...] = jnp.dot(
        left_part.astype(jnp.bfloat16),
        rr_ref[...].astype(jnp.bfloat16),
        preferred_element_type=f32,
    ).astype(jnp.bfloat16)
    writes[0].start()
    for write in writes:
        write.wait()


def finish(grad, left_stat, right_stat, left_root, right_root):
    vmem = pl.BlockSpec(memory_space=pltpu.VMEM)
    out_shape = [
        jax.ShapeDtypeStruct(grad.shape, jnp.bfloat16),
        jax.ShapeDtypeStruct(left_stat.shape, jnp.float32),
        jax.ShapeDtypeStruct(right_stat.shape, jnp.float32),
    ]
    return pl.pallas_call(
        finish_kernel,
        out_shape=out_shape,
        in_specs=[vmem] * 5,
        out_specs=[pl.BlockSpec(memory_space=pl.ANY)] * 3,
        scratch_shapes=[pltpu.VMEM(x.shape, x.dtype) for x in out_shape]
        + [pltpu.SemaphoreType.DMA((3,))],
        compiler_params=pltpu.CompilerParams(vmem_limit_bytes=16 * MIB),
        cost_estimate=pl.CostEstimate(flops=4 * 2 * 512**3, bytes_accessed=7 * MIB, transcendentals=0),
    )(grad, left_stat, right_stat, left_root, right_root)


def per_device(grad_parts, owner_of, refresh, left_stat, right_stat, left_root, right_root):
    n_owner = lax.axis_size("owner")
    n_slots = lax.axis_size("dp") * n_owner
    slot = (lax.axis_index("dp") * n_owner + lax.axis_index("owner")).reshape(1)
    shard_rows = grad_parts[0]
    streams = build_streams(n_owner // 2)
    counts = [2 * count for _, count, _ in streams]

    def send(x, *how):
        return lax.ppermute(x, AXES, route(n_slots, n_owner, *how))

    def steps(number, sent, other=0):
        return [send(x, orders, number, other) for (_, _, orders), x in zip(streams, sent)]

    def total(got, kept, token):
        arrays = [x for pair in zip(got, kept) for x in pair]
        parts = [(count, [(2 * k, 0), (2 * k + 1, 0)]) for k, count in enumerate(counts)]
        return event(arrays, [parts], (token,))[0]

    def to_owners(x):
        groups = [list(range(core, n_owner, 2)) for core in (0, 1)]
        x = x.reshape(n_owner // 2, -1, x.shape[2])
        x = lax.all_to_all(
            x, "owner", split_axis=0, concat_axis=0, tiled=True, axis_index_groups=groups
        )
        return x.reshape(-1, x.shape[2])

    plan = [[stream + (0, 1) for stream in streams]]
    plan += [[stream + (1, other)] for other in (0, 1) for stream in streams]
    handed, *sent, token = pick(slot, n_owner, owner_of, shard_rows, plan, chunks=CHUNKS)
    handed = send(handed, None, 0, 1)
    same, other = steps(0, sent[: len(streams)]), steps(0, sent[len(streams) :], 1)
    plan = [[stream + (0, 0)] for stream in streams]
    *own, token = pick(slot, n_owner, owner_of, shard_rows, plan, (token,))
    stats_and_roots = [x[0] for x in (left_stat, right_stat, left_root, right_root)]
    new_left_root, new_right_root, token = roots(
        owner_of, refresh, slot, stats_and_roots, token
    )
    places = [count for _, count, _ in streams]
    same = event(
        [x for pair in zip(same, own) for x in pair],
        [[(4 * n, [(2 * k, 0), (2 * k + 1, 0)])] for k, n in enumerate(places)],
        (token,),
    )
    arrays = [x for pair in zip(same, other) for x in pair]
    sent = first_sum(slot, places, 1, handed, arrays, same[0])
    got = steps(1, sent)
    kept = first_sum(slot, places, 0, handed, arrays, sent[0])

    def part(second):
        return [
            [(count, [(2 * k, second * count), (2 * k + 1, second * count)])]
            for k, count in enumerate(counts)
        ]

    arrays = [x for pair in zip(got, kept) for x in pair]
    sent = event(arrays, part(1), (kept[0],))
    got = steps(2, sent)
    kept = event(arrays, part(0), (sent[0],))
    token = kept[0]
    grad = total(got, kept, token)
    update, new_left, new_right = finish(to_owners(grad), *stats_and_roots)
    return (
        update[None],
        new_left[None],
        new_right[None],
        new_left_root[None],
        new_right_root[None],
    )


def solution(mesh):
    owned = P(AXES, None, None)
    return jax.shard_map(
        per_device,
        mesh=mesh,
        in_specs=(P("dp", None, "owner", None), P(), P(), owned, owned, owned, owned),
        out_specs=(owned,) * 5,
        check_vma=False,
    )
```
